32 devices in a mesh: dom: 8 (over z, y), lev: 4 (over x, core).
Axes of the slice: x: 2, y: 2, z: 4, core: 2. Of those that a mesh axis runs over, the one named last changes fastest.
Arguments:
- source: bfloat16 [8, 128, 16384], P(None, 'lev', 'dom'), may hold values from -6 to 6
- send_slots: int32 [8, 5, 4], P('dom'), may hold values from 0 to 15
- intersection_col: int32 [8, 32768], P(None, 'dom'), may hold values from 0 to 2559, as said below
- intersection_wt: float32 [8, 32768], P(None, 'dom'), may hold values from 0.05 to 1
- intersection_count: int32 [32768], P('dom'), may hold values from 1 to 8
- neighbours: int32 [6, 32768], P(None, 'dom'), may hold values from 0 to 4351, as said below
- land_mask: int32 [32768], P('dom'), may hold values 0 or 1
- diffusivity: float32 [8, 128], P(None, 'lev'), may hold values from 0.02 to 0.15
Outputs:
- updated: float32 [8, 128, 32768], P(None, 'lev', 'dom')
The draws below stay inside these ranges and needn't reach their ends.
Inputs may be any that keep to these rules, and one draw needn't show every extreme that they name: `intersection_col`: entries name columns of the target domain's received set; the 8 entries of one target cell name different columns. `neighbours`: a neighbour lies within 128 cells of its cell in the cyclic global cell order; the entry is its position among the domain's cells preceded and followed by 128 cells of the adjacent domains.
All inputs are finite; a program needn't handle non-finite values. No bound on the sum of `land_mask` on one device may be relied on, other than what follows from the above.
Results may differ from the reference program's by a relative error of at most 0.0024.
Values may be sent and summed in bfloat16 or wider, within the bound.
A program may use at most 64 MiB of HBM per device.

```python
import math
import jax
import jax.numpy as jnp
from jax import lax

F = 8
L = 128
B = 128
SB = 16
CAP = 4
R = 2
K = 8
NN = 6
H = 128
TGT_DEV = 4096
NDOMS = 8
NS = 16384
NT = 32768
N_DOM = 8


def draw_intersection_col(key, part):
    key = jax.random.fold_in(key, 11)
    first_key, second_key = jax.random.split(key)
    width = (2 * R + 1) * CAP * B
    stride = width // K
    base = jax.random.randint(first_key, (1, TGT_DEV * N_DOM), 0, width)
    jitter = jax.random.randint(second_key, (K, TGT_DEV * N_DOM), 0, stride)
    slots = jnp.arange(K, dtype=jnp.int32)[:, None]
    return ((base + slots * stride + jitter) % width).astype(jnp.int32)


def draw_neighbours(key, part):
    key = jax.random.fold_in(key, 23)
    shifts = jax.random.randint(key, (NN, TGT_DEV * N_DOM), -H, H + 1)
    local = jnp.arange(TGT_DEV * N_DOM, dtype=jnp.int32)[None, :] % TGT_DEV
    rows = jnp.arange(NN, dtype=jnp.int32)[:, None]
    shifts = jnp.where((rows == 0) & (local == 0), -H, shifts)
    shifts = jnp.where((rows == 0) & (local == TGT_DEV - 1), H, shifts)
    return (local + H + shifts).astype(jnp.int32)


def set_ends(result, key, least, top_value):
    place = [jax.random.randint(jax.random.fold_in(key, axis), (), 0, length) for axis, length in enumerate(result.shape)]
    widest = result.shape.index(max(result.shape))
    next_to = place[:widest] + [(place[widest] + 1) % result.shape[widest]] + place[widest + 1:]
    return result.at[tuple(place)].set(least).at[tuple(next_to)].set(top_value)


def shard_levels(stream_key, dims, pieces, least, top_value):
    factor_of = 1.0
    for position, parts in pieces:
        heights = jax.random.uniform(jax.random.fold_in(jax.random.fold_in(stream_key, 6), position), (parts,), jnp.float32, least / len(pieces), top_value / len(pieces))
        factor_of = factor_of * jnp.repeat(jnp.exp(heights), dims[position] // parts).reshape((-1,) + (1,) * (len(dims) - 1 - position))
    return factor_of


def noise(key, extent, deviation, reach, shards=(), held_as=jnp.bfloat16):
    array = deviation * jax.random.normal(key, extent, jnp.float32)
    if shards:
        array = array * shard_levels(key, extent, shards, -0.22, 0.18)
    return jnp.clip(array, -reach, reach).astype(held_as)


def setup_inputs(seed: int = 0) -> dict:
    keys = jax.random.split(jax.random.key(seed), 9)
    return {
        "source": noise(keys[0], (F, L, NS), 1.0, 6.0, ((1, 4), (2, 8))),
        "send_slots": set_ends(jax.random.randint(keys[1], (NDOMS, 2 * R + 1, CAP), 0, SB), jax.random.fold_in(keys[1], 1), 0, SB - 1).astype(jnp.int32),
        "intersection_col": draw_intersection_col(jax.random.fold_in(keys[8], 71), 0),
        "intersection_wt": jnp.clip(jnp.exp(math.log(1.0) - 2.9957323 * jax.random.uniform(keys[3], (K, NT), jnp.float32) ** shard_levels(keys[3], (K, NT), ((1, 8),), -0.2, 0.2)), 0.05, 1.0),
        "intersection_count": set_ends(jax.random.randint(keys[4], (NT,), 1, K + 1), jax.random.fold_in(keys[4], 1), 1, K).astype(jnp.int32),
        "neighbours": draw_neighbours(jax.random.fold_in(keys[8], 71), 0),
        "land_mask": set_ends((jax.random.randint(keys[6], (NT,), 0, 4) < 3).astype(jnp.int32), jax.random.fold_in(keys[6], 1), 0, 1),
        "diffusivity": jnp.clip(0.02 + 0.13000001 * jax.random.uniform(keys[7], (F, L), jnp.float32) ** shard_levels(keys[7], (F, L), ((1, 4),), -0.2, 0.2), 0.02, 0.15),
    }


vertical_rate = 0.1


def reference(source, send_slots, intersection_col, intersection_wt, intersection_count, neighbours, land_mask, diffusivity):
    slot_index = jnp.arange(K, dtype=jnp.int32)[:, None]
    live_wt = jnp.where(slot_index < intersection_count[None, :], intersection_wt, jnp.float32(0.0))
    shares = (live_wt / jnp.sum(live_wt, axis=0, keepdims=True)).astype(jnp.bfloat16)
    offsets = jnp.arange(2 * R + 1, dtype=jnp.int32)
    within = jnp.arange(B, dtype=jnp.int32)

    def remap_domain(domain):
        sender = ((domain - offsets + R) % N_DOM).astype(jnp.int32)
        chosen = send_slots[sender, offsets]
        columns_all = (sender[:, None, None] * (SB * B) + chosen[:, :, None] * B + within[None, None, :]).reshape(-1).astype(jnp.int32)
        received = jnp.take(source, columns_all, axis=2)
        start = (domain * TGT_DEV).astype(jnp.int32)
        block_cols = lax.dynamic_slice_in_dim(intersection_col, start, TGT_DEV, 1)
        block_shares = lax.dynamic_slice_in_dim(shares, start, TGT_DEV, 1)
        total = jnp.zeros((source.shape[0], source.shape[1], TGT_DEV), jnp.float32)
        for slot in range(K):
            picked = jnp.take(received, block_cols[slot], axis=2).astype(jnp.float32)
            total = total + picked * block_shares[slot].astype(jnp.float32)[None, None, :]
        return total

    remapped_all = lax.map(remap_domain, jnp.arange(N_DOM, dtype=jnp.int32))
    remapped = jnp.moveaxis(remapped_all, 0, 2).reshape(source.shape[0], source.shape[1], NT)
    ocean = land_mask.astype(jnp.float32)
    positions = jnp.arange(NT, dtype=jnp.int32)
    starts = positions - positions % TGT_DEV
    lateral = jnp.zeros_like(remapped)
    for neighbour in range(NN):
        global_ids = ((starts + neighbours[neighbour] - H) % NT).astype(jnp.int32)
        lateral = lateral + ocean[global_ids][None, None, :] * (remapped[:, :, global_ids] - remapped)
    padded = jnp.pad(remapped, ((0, 0), (1, 1), (0, 0)))
    vertical = padded[:, 2:, :] + padded[:, :-2, :] - 2.0 * remapped
    return ocean[None, None, :] * (remapped + diffusivity[:, :, None] * lateral + vertical_rate * vertical)
```

```python
import functools

import jax
import jax.numpy as jnp
from jax import lax
from jax.experimental import pallas as pl
from jax.experimental.pallas import tpu as pltpu
from jax.sharding import PartitionSpec as P

B = 128
CAP = 4
R = 2
K = 8
NN = 6
H = 128
OFFS = 2 * R + 1
SET = CAP * B
HALF = 256
TILE = 256
MESH = pl.DeviceIdType.MESH
vertical_rate = 0.1
ORDER = (R + 1, R - 1, R + 2, R - 2)


def kernel(
    fields,
    levels,
    slots_ref,
    src_ref,
    col_ref,
    wt_ref,
    cnt_ref,
    near_ref,
    land_ref,
    diff_ref,
    out_ref,
    blocks,
    outbox,
    inbox,
    d0,
    d1,
    d2,
    d3,
    d4,
    wref,
    share_ref,
    rref,
    xm,
    tri_ref,
    dref,
    lev_out,
    lev_in,
    send_sem,
    recv_sem,
    halo_send,
    halo_recv,
    lev_send,
    lev_recv,
    out_sem,
):
    dense = (d0, d1, d2, d3, d4)
    rows = fields * levels
    targets = land_ref.shape[1]
    tiles = targets // TILE
    f32, bf16 = jnp.float32, jnp.bfloat16
    nd = lax.axis_size("dom")
    nl = lax.axis_size("lev")
    me = lax.axis_index("dom")
    lev = lax.axis_index("lev")

    def at(step):
        return lax.rem(me + step + nd, nd)

    barrier = pltpu.get_barrier_semaphore()
    for step in (-2, -1, 1, 2):
        pl.semaphore_signal(barrier, inc=1, device_id=(at(step), lev), device_id_type=MESH)

    @pl.when(lev > 0)
    def _():
        pl.semaphore_signal(barrier, inc=1, device_id=(me, lev - 1), device_id_type=MESH)

    @pl.when(lev < nl - 1)
    def _():
        pl.semaphore_signal(barrier, inc=1, device_id=(me, lev + 1), device_id_type=MESH)

    def pick(offset):
        for c in range(CAP):
            slot = slots_ref[0, offset, c]
            outbox[offset, :, c * B : (c + 1) * B] = blocks[slot]

    for block in range(src_ref.shape[1] // B):
        blocks[block] = src_ref[:, block * B : (block + 1) * B]
    for offset in ORDER:
        pick(offset)
    beside_count = jnp.where(lev > 0, 1, 0) + jnp.where(lev < nl - 1, 1, 0)
    pl.semaphore_wait(barrier, 4 + beside_count)

    copies = []
    for i, offset in enumerate(ORDER):
        copy = pltpu.make_async_remote_copy(
            src_ref=outbox.at[offset],
            dst_ref=inbox.at[i],
            send_sem=send_sem.at[i],
            recv_sem=recv_sem.at[i],
            device_id=(at(offset - R), lev),
            device_id_type=MESH,
        )
        copy.start()
        copies.append(copy)
    pick(R)

    slot_ids = lax.broadcasted_iota(jnp.int32, (K, targets), 0)
    live = jnp.where(slot_ids < cnt_ref[...], wt_ref[...], 0.0)
    share_ref[...] = (live / jnp.sum(live, axis=0, keepdims=True)).astype(bf16).astype(f32)

    row16 = lax.broadcasted_iota(jnp.int32, (16, B), 0).astype(f32)

    def strip_of(s):
        return pl.ds(pl.multiple_of(s * B, B), B)

    def build(offset, s):
        target = dense[offset]
        lanes = strip_of(s)
        col = col_ref[:, lanes].astype(f32)
        share = share_ref[:, lanes]
        shares = [jnp.broadcast_to(share[k : k + 1], (16, B)).astype(bf16) for k in range(K)]
        for h in range(SET // HALF):
            base = float(offset * SET + h * HALF)
            places = [
                jnp.broadcast_to(col[k : k + 1] - base, (16, B)).astype(bf16) for k in range(K)
            ]
            for i in range(HALF // 16):
                ids = (row16 + float(16 * i)).astype(bf16)
                acc = jnp.zeros((16, B), bf16)
                for k in range(K):
                    acc = jnp.where(places[k] == ids, shares[k], acc)
                start = h * HALF + 16 * i
                target[start : start + 16, lanes] = acc

    def build_near(s):
        lanes = strip_of(s)
        start = (s // (TILE // B)) * TILE
        near = (near_ref[:, lanes] - start).astype(f32)
        one = jnp.ones((16, B), bf16)
        for h in range(2):
            places = [
                jnp.broadcast_to(near[n : n + 1] - float(h * HALF), (16, B)).astype(bf16)
                for n in range(NN)
            ]
            for i in range(HALF // 16):
                ids = (row16 + float(16 * i)).astype(bf16)
                acc = jnp.zeros((16, B), bf16)
                for n in range(NN):
                    acc = jnp.where(places[n] == ids, acc + one, acc)
                at_row = h * HALF + 16 * i
                wref[at_row : at_row + 16, lanes] = acc

    def tile_of(j, shift=0, width=TILE):
        return pl.ds(pl.multiple_of(j * TILE + shift, B), width)

    def product(offset, j):
        left = outbox[R] if offset == R else inbox[ORDER.index(offset)]
        return jnp.dot(left, dense[offset][:, tile_of(j)], preferred_element_type=f32)

    def loop(body, low, high):
        lax.fori_loop(low, high, lambda j, c: (body(j), c)[1], 0)

    both = TILE // B

    def build_tile(offset, j):
        for p in range(both):
            build(offset, j * both + p)

    def near_tile(j):
        for p in range(both):
            build_near(j * both + p)

    for part in range(rows // TILE):
        row_id = lax.broadcasted_iota(jnp.int32, (TILE, rows), 0) + part * TILE
        col_id = lax.broadcasted_iota(jnp.int32, (TILE, rows), 1)
        beside = (jnp.abs(row_id - col_id) == 1) & (row_id // levels == col_id // levels)
        tri_ref[part * TILE : (part + 1) * TILE, :] = jnp.where(beside, 1.0, 0.0).astype(bf16)
    lane_id = lax.broadcasted_iota(jnp.int32, (levels, levels), 1)
    level_id = lax.broadcasted_iota(jnp.int32, (levels, levels), 0)
    for f in range(fields):
        spread = jnp.broadcast_to(diff_ref[f : f + 1, :], (levels, levels))
        column = jnp.sum(jnp.where(lane_id == level_id, spread, 0.0), axis=1, keepdims=True)
        dref[f * levels : (f + 1) * levels, :] = jnp.broadcast_to(column, (levels, TILE))
    first_row = lax.broadcasted_iota(jnp.int32, (16, targets), 0) == 0
    ocean_row = jnp.broadcast_to(land_ref[...].astype(f32), (16, targets))
    xm[rows:, H : H + targets] = jnp.where(first_row, ocean_row, 0.0).astype(bf16)

    def own_first(j):
        rref[:, tile_of(j)] = product(R, j)
        build_tile(ORDER[0], j)

    def add_and_build(offset, following):
        def body(j):
            rref[:, tile_of(j)] += product(offset, j)
            build_tile(following, j)

        return body

    def add(offset):
        def body(j):
            rref[:, tile_of(j)] += product(offset, j)

        return body

    loop(lambda j: build_tile(R, j), 0, tiles)
    loop(own_first, 0, tiles)
    loop(near_tile, 0, tiles)
    loop(lambda j: build_tile(ORDER[1], j), 0, tiles)
    copies[0].wait_recv()
    loop(add_and_build(ORDER[0], ORDER[2]), 0, tiles)
    copies[1].wait_recv()
    loop(add_and_build(ORDER[1], ORDER[3]), 0, tiles)
    copies[2].wait_recv()
    loop(add(ORDER[2]), 0, tiles)
    copies[3].wait_recv()

    def last(j):
        value = rref[:, tile_of(j)] + product(ORDER[3], j)
        rref[:, tile_of(j)] = value
        ocean = land_ref[:, tile_of(j)].astype(f32)
        xm[:rows, tile_of(j, H)] = (value * ocean).astype(bf16)
        for side, level in ((0, levels - 1), (1, 0)):
            picked = [
                rref[f * levels + level : f * levels + level + 1, tile_of(j, p * B, B)]
                for p in range(both)
                for f in range(fields)
            ]
            lev_out[side, :, strip_of(j)] = jnp.concatenate(picked, axis=0).astype(bf16)

    last(0)
    last(tiles - 1)
    halos = []
    for i, (start, landing, step) in enumerate(
        ((targets, 0, 1), (H, H + targets, -1))
    ):
        copy = pltpu.make_async_remote_copy(
            src_ref=xm.at[:, pl.ds(start, H)],
            dst_ref=xm.at[:, pl.ds(landing, H)],
            send_sem=halo_send.at[i],
            recv_sem=halo_recv.at[i],
            device_id=(at(step), lev),
            device_id_type=MESH,
        )
        copy.start()
        halos.append(copy)
    loop(last, 1, tiles - 1)

    def level_copy(side):
        return pltpu.make_async_remote_copy(
            src_ref=lev_out.at[side],
            dst_ref=lev_in.at[side],
            send_sem=lev_send.at[side],
            recv_sem=lev_recv.at[side],
            device_id=(me, lev + 1 if side == 0 else lev - 1),
            device_id_type=MESH,
        )

    @pl.when(lev < nl - 1)
    def _():
        level_copy(0).start()

    @pl.when(lev > 0)
    def _():
        level_copy(1).start()

    @pl.when(lev == 0)
    def _():
        lev_in[0] = jnp.zeros(lev_in.shape[1:], bf16)

    @pl.when(lev == nl - 1)
    def _():
        lev_in[1] = jnp.zeros(lev_in.shape[1:], bf16)

    def final(j):
        gathered = jnp.dot(
            xm[:, tile_of(j, 0, 2 * TILE)], wref[:, tile_of(j)], preferred_element_type=f32
        )
        value = rref[:, tile_of(j)]
        beside = jnp.dot(tri_ref[...], value.astype(bf16), preferred_element_type=f32)
        d = dref[...]
        total = gathered[rows : rows + 1]
        rref[:, tile_of(j)] = (
            value * ((1.0 - 2.0 * vertical_rate) - d * total)
            + d * gathered[:rows]
            + vertical_rate * beside
        )

    def out_copy(j):
        return pltpu.make_async_copy(
            rref.at[:, tile_of(j)], out_ref.at[:, tile_of(j)], out_sem.at[j]
        )

    def edges(j):
        for side, level in ((0, 0), (1, levels - 1)):
            part = lev_in[side, :, strip_of(j)].astype(f32)
            for p in range(both):
                for f in range(fields):
                    row = f * levels + level
                    at_part = p * fields + f
                    edge = part[at_part : at_part + 1]
                    rref[row : row + 1, tile_of(j, p * B, B)] += vertical_rate * edge
        out_copy(j).start()

    loop(final, 1, tiles - 1)
    for copy in halos:
        copy.wait_recv()
    for copy in halos:
        copy.wait_send()
    final(0)
    final(tiles - 1)

    @pl.when(lev > 0)
    def _():
        level_copy(0).wait_recv()
        level_copy(1).wait_send()

    @pl.when(lev < nl - 1)
    def _():
        level_copy(1).wait_recv()
        level_copy(0).wait_send()

    loop(edges, 0, tiles)
    for copy in copies:
        copy.wait_send()
    loop(lambda j: out_copy(j).wait(), 0, tiles)


def on_device(
    source,
    send_slots,
    intersection_col,
    intersection_wt,
    intersection_count,
    neighbours,
    land_mask,
    diffusivity,
):
    fields, levels, columns = source.shape
    rows = fields * levels
    targets = land_mask.shape[0]
    f32, bf16 = jnp.float32, jnp.bfloat16
    vmem = pl.BlockSpec(memory_space=pltpu.VMEM)
    land = land_mask.reshape(1, targets)
    result = pl.pallas_call(
        functools.partial(kernel, fields, levels),
        out_shape=jax.ShapeDtypeStruct((rows, targets), f32),
        in_specs=[pl.BlockSpec(memory_space=pltpu.SMEM)] + [vmem] * 7,
        out_specs=pl.BlockSpec(memory_space=pl.ANY),
        scratch_shapes=[
            pltpu.VMEM((columns // B, rows, B), bf16),
            pltpu.VMEM((OFFS, rows, SET), bf16),
            pltpu.VMEM((OFFS - 1, rows, SET), bf16),
        ]
        + [pltpu.VMEM((SET, targets), bf16) for _ in range(OFFS)]
        + [
            pltpu.VMEM((2 * TILE, targets), bf16),
            pltpu.VMEM((K, targets), f32),
            pltpu.VMEM((rows, targets), f32),
            pltpu.VMEM((rows + 16, targets + 2 * H), bf16),
            pltpu.VMEM((rows, rows), bf16),
            pltpu.VMEM((rows, TILE), f32),
            pltpu.VMEM((2, 2 * fields, targets // 2), bf16),
            pltpu.VMEM((2, 2 * fields, targets // 2), bf16),
            pltpu.SemaphoreType.DMA((OFFS - 1,)),
            pltpu.SemaphoreType.DMA((OFFS - 1,)),
            pltpu.SemaphoreType.DMA((2,)),
            pltpu.SemaphoreType.DMA((2,)),
            pltpu.SemaphoreType.DMA((2,)),
            pltpu.SemaphoreType.DMA((2,)),
            pltpu.SemaphoreType.DMA((targets // TILE,)),
        ],
        compiler_params=pltpu.CompilerParams(
            collective_id=0, has_side_effects=True, vmem_limit_bytes=48 * 1024 * 1024
        ),
    )(
        send_slots,
        source.reshape(rows, columns),
        intersection_col,
        intersection_wt,
        intersection_count.reshape(1, targets),
        neighbours,
        land,
        diffusivity,
    )
    updated = land.astype(f32) * result
    return updated.reshape(fields, levels, targets)


def solution(mesh):
    return jax.shard_map(
        on_device,
        mesh=mesh,
        in_specs=(
            P(None, "lev", "dom"),
            P("dom", None, None),
            P(None, "dom"),
            P(None, "dom"),
            P("dom"),
            P(None, "dom"),
            P("dom"),
            P(None, "lev"),
        ),
        out_specs=P(None, "lev", "dom"),
        check_vma=False,
    )
```

```python
import functools

import jax
import jax.numpy as jnp
from jax import lax
from jax.experimental import pallas as pl
from jax.experimental.pallas import tpu as pltpu
from jax.sharding import PartitionSpec as P

B = 128
CAP = 4
R = 2
K = 8
NN = 6
H = 128
OFFS = 2 * R + 1
SET = CAP * B
HALF = 256
TILE = 256
MESH = pl.DeviceIdType.MESH
vertical_rate = 0.1
ORDER = (R + 1, R - 1, R + 2, R - 2)


def kernel(
    fields,
    levels,
    slots_hbm,
    src_hbm,
    col_hbm,
    wt_hbm,
    cnt_hbm,
    near_hbm,
    land_hbm,
    diff_hbm,
    out_ref,
    slots_ref,
    src_ref,
    col_ref,
    wt_ref,
    cnt_ref,
    near_ref,
    land_ref,
    diff_ref,
    in_sem,
    blocks,
    outbox,
    inbox,
    own_dense,
    near_dense,
    far_dense,
    wref,
    share_ref,
    rref,
    xm,
    tri_ref,
    dref,
    lev_out,
    lev_in,
    send_sem,
    recv_sem,
    halo_send,
    halo_recv,
    lev_send,
    lev_recv,
    out_sem,
):
    loads = []
    for i, (hbm, ref) in enumerate(
        (
            (src_hbm, src_ref),
            (slots_hbm, slots_ref),
            (col_hbm, col_ref),
            (wt_hbm, wt_ref),
            (cnt_hbm, cnt_ref),
            (near_hbm, near_ref),
            (land_hbm, land_ref),
            (diff_hbm, diff_ref),
        )
    ):
        load = pltpu.make_async_copy(hbm, ref, in_sem.at[i])
        load.start()
        loads.append(load)
    dense = {R: (own_dense, 0)}
    for i, offset in enumerate(ORDER):
        dense[offset] = ((near_dense, far_dense)[i // 2], (i % 2) * SET)
    rows = fields * levels
    targets = land_ref.shape[1]
    tiles = targets // TILE
    f32, bf16 = jnp.float32, jnp.bfloat16
    nd = lax.axis_size("dom")
    nl = lax.axis_size("lev")
    me = lax.axis_index("dom")
    lev = lax.axis_index("lev")

    def at(step):
        return lax.rem(me + step + nd, nd)

    barrier = pltpu.get_barrier_semaphore()
    for step in (-2, -1, 1, 2):
        pl.semaphore_signal(barrier, inc=1, device_id=(at(step), lev), device_id_type=MESH)

    @pl.when(lev > 0)
    def _():
        pl.semaphore_signal(barrier, inc=1, device_id=(me, lev - 1), device_id_type=MESH)

    @pl.when(lev < nl - 1)
    def _():
        pl.semaphore_signal(barrier, inc=1, device_id=(me, lev + 1), device_id_type=MESH)

    def pick(offset):
        for c in range(CAP):
            slot = slots_ref[0, offset, c]
            outbox[offset, :, c * B : (c + 1) * B] = blocks[slot]

    loads[0].wait()
    loads[1].wait()
    for block in range(src_ref.shape[1] // B):
        blocks[block] = src_ref[:, block * B : (block + 1) * B]
    for offset in ORDER:
        pick(offset)
    beside_count = jnp.where(lev > 0, 1, 0) + jnp.where(lev < nl - 1, 1, 0)
    pl.semaphore_wait(barrier, 4 + beside_count)

    copies = []
    for i, offset in enumerate(ORDER):
        copy = pltpu.make_async_remote_copy(
            src_ref=outbox.at[offset],
            dst_ref=inbox.at[i // 2, :, pl.ds((i % 2) * SET, SET)],
            send_sem=send_sem.at[i],
            recv_sem=recv_sem.at[i],
            device_id=(at(offset - R), lev),
            device_id_type=MESH,
        )
        copy.start()
        copies.append(copy)
    pick(R)

    for load in loads[2:]:
        load.wait()
    slot_ids = lax.broadcasted_iota(jnp.int32, (K, targets), 0)
    live = jnp.where(slot_ids < cnt_ref[...], wt_ref[...], 0.0)
    share_ref[...] = (live / jnp.sum(live, axis=0, keepdims=True)).astype(bf16).astype(f32)

    row16 = lax.broadcasted_iota(jnp.int32, (16, B), 0).astype(f32)

    def strip_of(s):
        return pl.ds(pl.multiple_of(s * B, B), B)

    def build(offset, s):
        target, low_row = dense[offset]
        lanes = strip_of(s)
        col = col_ref[:, lanes].astype(f32)
        share = share_ref[:, lanes]
        shares = [jnp.broadcast_to(share[k : k + 1], (16, B)).astype(bf16) for k in range(K)]
        for h in range(SET // HALF):
            base = float(offset * SET + h * HALF)
            places = [
                jnp.broadcast_to(col[k : k + 1] - base, (16, B)).astype(bf16) for k in range(K)
            ]
            for i in range(HALF // 16):
                ids = (row16 + float(16 * i)).astype(bf16)
                acc = jnp.zeros((16, B), bf16)
                for k in range(K):
                    acc = jnp.where(places[k] == ids, shares[k], acc)
                start = low_row + h * HALF + 16 * i
                target[start : start + 16, lanes] = acc

    def build_near(s):
        lanes = strip_of(s)
        start = (s // (TILE // B)) * TILE
        near = (near_ref[:, lanes] - start).astype(f32)
        one = jnp.ones((16, B), bf16)
        for h in range(2):
            places = [
                jnp.broadcast_to(near[n : n + 1] - float(h * HALF), (16, B)).astype(bf16)
                for n in range(NN)
            ]
            for i in range(HALF // 16):
                ids = (row16 + float(16 * i)).astype(bf16)
                acc = jnp.zeros((16, B), bf16)
                for n in range(NN):
                    acc = jnp.where(places[n] == ids, acc + one, acc)
                at_row = h * HALF + 16 * i
                wref[at_row : at_row + 16, lanes] = acc

    def tile_of(j, shift=0, width=TILE):
        return pl.ds(pl.multiple_of(j * TILE + shift, B), width)

    def product(part, j):
        if part == 0:
            left, right = outbox[R], own_dense
        else:
            left, right = inbox[part - 1], (near_dense, far_dense)[part - 1]
        return jnp.dot(left, right[:, tile_of(j)], preferred_element_type=f32)

    def loop(body, low, high, group=1):
        def step(i, carry):
            for p in range(group):
                body(low + i * group + p)
            return carry

        lax.fori_loop(0, (high - low) // group, step, 0)

    both = TILE // B

    def build_tile(offset, j):
        for p in range(both):
            build(offset, j * both + p)

    def near_tile(j):
        for p in range(both):
            build_near(j * both + p)

    for part in range(rows // TILE):
        row_id = lax.broadcasted_iota(jnp.int32, (TILE, rows), 0) + part * TILE
        col_id = lax.broadcasted_iota(jnp.int32, (TILE, rows), 1)
        beside = (jnp.abs(row_id - col_id) == 1) & (row_id // levels == col_id // levels)
        tri_ref[part * TILE : (part + 1) * TILE, :] = jnp.where(beside, 1.0, 0.0).astype(bf16)
    lane_id = lax.broadcasted_iota(jnp.int32, (levels, levels), 1)
    level_id = lax.broadcasted_iota(jnp.int32, (levels, levels), 0)
    for f in range(fields):
        spread = jnp.broadcast_to(diff_ref[f : f + 1, :], (levels, levels))
        column = jnp.sum(jnp.where(lane_id == level_id, spread, 0.0), axis=1, keepdims=True)
        dref[f * levels : (f + 1) * levels, :] = jnp.broadcast_to(column, (levels, TILE))
    first_row = lax.broadcasted_iota(jnp.int32, (16, targets), 0) == 0
    ocean_row = jnp.broadcast_to(land_ref[...].astype(f32), (16, targets))
    xm[rows:, H : H + targets] = jnp.where(first_row, ocean_row, 0.0).astype(bf16)

    def own_first(j):
        rref[:, tile_of(j)] = product(0, j)
        build_tile(ORDER[0], j)

    def second(j):
        rref[:, tile_of(j)] += product(1, j)
        build_tile(ORDER[3], j)

    loop(lambda j: build_tile(R, j), 0, tiles)
    loop(own_first, 0, tiles, 2)
    loop(near_tile, 0, tiles)
    loop(lambda j: build_tile(ORDER[1], j), 0, tiles)
    loop(lambda j: build_tile(ORDER[2], j), 0, tiles)
    copies[0].wait_recv()
    copies[1].wait_recv()
    loop(second, 0, tiles, 2)
    copies[2].wait_recv()
    copies[3].wait_recv()

    def last(j):
        value = rref[:, tile_of(j)] + product(2, j)
        rref[:, tile_of(j)] = value
        ocean = land_ref[:, tile_of(j)].astype(f32)
        xm[:rows, tile_of(j, H)] = (value * ocean).astype(bf16)
        for side, level in ((0, levels - 1), (1, 0)):
            picked = [
                rref[f * levels + level : f * levels + level + 1, tile_of(j, p * B, B)]
                for p in range(both)
                for f in range(fields)
            ]
            lev_out[side, :, strip_of(j)] = jnp.concatenate(picked, axis=0).astype(bf16)

    last(0)
    last(tiles - 1)
    halos = []
    for i, (start, landing, step) in enumerate(
        ((targets, 0, 1), (H, H + targets, -1))
    ):
        copy = pltpu.make_async_remote_copy(
            src_ref=xm.at[:, pl.ds(start, H)],
            dst_ref=xm.at[:, pl.ds(landing, H)],
            send_sem=halo_send.at[i],
            recv_sem=halo_recv.at[i],
            device_id=(at(step), lev),
            device_id_type=MESH,
        )
        copy.start()
        halos.append(copy)
    loop(last, 1, tiles - 1, 2)

    def level_copy(side):
        return pltpu.make_async_remote_copy(
            src_ref=lev_out.at[side],
            dst_ref=lev_in.at[side],
            send_sem=lev_send.at[side],
            recv_sem=lev_recv.at[side],
            device_id=(me, lev + 1 if side == 0 else lev - 1),
            device_id_type=MESH,
        )

    @pl.when(lev < nl - 1)
    def _():
        level_copy(0).start()

    @pl.when(lev > 0)
    def _():
        level_copy(1).start()

    @pl.when(lev == 0)
    def _():
        lev_in[0] = jnp.zeros(lev_in.shape[1:], bf16)

    @pl.when(lev == nl - 1)
    def _():
        lev_in[1] = jnp.zeros(lev_in.shape[1:], bf16)

    def final(j):
        gathered = jnp.dot(
            xm[:, tile_of(j, 0, 2 * TILE)], wref[:, tile_of(j)], preferred_element_type=f32
        )
        value = rref[:, tile_of(j)]
        beside = jnp.dot(tri_ref[...], value.astype(bf16), preferred_element_type=f32)
        d = dref[...]
        total = gathered[rows : rows + 1]
        rref[:, tile_of(j)] = (
            value * ((1.0 - 2.0 * vertical_rate) - d * total)
            + d * gathered[:rows]
            + vertical_rate * beside
        )

    def out_copy(j):
        return pltpu.make_async_copy(
            rref.at[:, tile_of(j)], out_ref.at[:, tile_of(j)], out_sem.at[j]
        )

    def edges(j):
        for side, level in ((0, 0), (1, levels - 1)):
            part = lev_in[side, :, strip_of(j)].astype(f32)
            for p in range(both):
                for f in range(fields):
                    row = f * levels + level
                    at_part = p * fields + f
                    edge = part[at_part : at_part + 1]
                    rref[row : row + 1, tile_of(j, p * B, B)] += vertical_rate * edge
        out_copy(j).start()

    middle = tiles // 2 - 1
    loop(final, 1, middle, 2)

    @pl.when(lev > 0)
    def _():
        level_copy(0).wait_recv()
        level_copy(1).wait_send()

    @pl.when(lev < nl - 1)
    def _():
        level_copy(1).wait_recv()
        level_copy(0).wait_send()

    def finish(j):
        final(j)
        edges(j)

    loop(edges, 1, middle)
    loop(finish, middle, tiles - 1, 2)
    for copy in halos:
        copy.wait_recv()
    for copy in halos:
        copy.wait_send()
    finish(0)
    finish(tiles - 1)
    for copy in copies:
        copy.wait_send()
    loop(lambda j: out_copy(j).wait(), 0, tiles)


def on_device(
    source,
    send_slots,
    intersection_col,
    intersection_wt,
    intersection_count,
    neighbours,
    land_mask,
    diffusivity,
):
    fields, levels, columns = source.shape
    rows = fields * levels
    targets = land_mask.shape[0]
    f32, bf16 = jnp.float32, jnp.bfloat16
    land = land_mask.reshape(1, targets)
    result = pl.pallas_call(
        functools.partial(kernel, fields, levels),
        out_shape=jax.ShapeDtypeStruct((rows, targets), f32),
        in_specs=[pl.BlockSpec(memory_space=pltpu.HBM)] * 8,
        out_specs=pl.BlockSpec(memory_space=pl.ANY),
        scratch_shapes=[
            pltpu.SMEM(send_slots.shape, jnp.int32),
            pltpu.VMEM((rows, columns), bf16),
            pltpu.VMEM((K, targets), jnp.int32),
            pltpu.VMEM((K, targets), f32),
            pltpu.VMEM((1, targets), jnp.int32),
            pltpu.VMEM((NN, targets), jnp.int32),
            pltpu.VMEM((1, targets), jnp.int32),
            pltpu.VMEM((fields, levels), f32),
            pltpu.SemaphoreType.DMA((8,)),
            pltpu.VMEM((columns // B, rows, B), bf16),
            pltpu.VMEM((OFFS, rows, SET), bf16),
            pltpu.VMEM((2, rows, 2 * SET), bf16),
            pltpu.VMEM((SET, targets), bf16),
            pltpu.VMEM((2 * SET, targets), bf16),
            pltpu.VMEM((2 * SET, targets), bf16),
            pltpu.VMEM((2 * TILE, targets), bf16),
            pltpu.VMEM((K, targets), f32),
            pltpu.VMEM((rows, targets), f32),
            pltpu.VMEM((rows + 16, targets + 2 * H), bf16),
            pltpu.VMEM((rows, rows), bf16),
            pltpu.VMEM((rows, TILE), f32),
            pltpu.VMEM((2, 2 * fields, targets // 2), bf16),
            pltpu.VMEM((2, 2 * fields, targets // 2), bf16),
            pltpu.SemaphoreType.DMA((OFFS - 1,)),
            pltpu.SemaphoreType.DMA((OFFS - 1,)),
            pltpu.SemaphoreType.DMA((2,)),
            pltpu.SemaphoreType.DMA((2,)),
            pltpu.SemaphoreType.DMA((2,)),
            pltpu.SemaphoreType.DMA((2,)),
            pltpu.SemaphoreType.DMA((targets // TILE,)),
        ],
        compiler_params=pltpu.CompilerParams(
            collective_id=0, has_side_effects=True, vmem_limit_bytes=64 * 1024 * 1024
        ),
    )(
        send_slots,
        source.reshape(rows, columns),
        intersection_col,
        intersection_wt,
        intersection_count.reshape(1, targets),
        neighbours,
        land,
        diffusivity,
    )
    updated = land.astype(f32) * result
    return updated.reshape(fields, levels, targets)


def solution(mesh):
    return jax.shard_map(
        on_device,
        mesh=mesh,
        in_specs=(
            P(None, "lev", "dom"),
            P("dom", None, None),
            P(None, "dom"),
            P(None, "dom"),
            P("dom"),
            P(None, "dom"),
            P("dom"),
            P(None, "lev"),
        ),
        out_specs=P(None, "lev", "dom"),
        check_vma=False,
    )
```

```python
import functools

import jax
import jax.numpy as jnp
from jax import lax
from jax.experimental import pallas as pl
from jax.experimental.pallas import tpu as pltpu
from jax.sharding import PartitionSpec as P

B = 128
CAP = 4
R = 2
K = 8
NN = 6
H = 128
OFFS = 2 * R + 1
SET = CAP * B
HALF = 256
TILE = 256
MESH = pl.DeviceIdType.MESH
vertical_rate = 0.1
ORDER = (R + 1, R - 1, R + 2, R - 2)


def kernel(
    fields,
    levels,
    slots_hbm,
    src_hbm,
    col_hbm,
    wt_hbm,
    cnt_hbm,
    near_hbm,
    land_hbm,
    diff_hbm,
    out_ref,
    slots_ref,
    src_ref,
    col_ref,
    wt_ref,
    cnt_ref,
    near_ref,
    land_ref,
    diff_ref,
    in_sem,
    blocks,
    outbox,
    inbox,
    own_dense,
    near_dense,
    far_dense,
    wref,
    share_ref,
    rref,
    qref,
    xm,
    tri_ref,
    dref,
    lev_out,
    lev_in,
    send_sem,
    recv_sem,
    halo_send,
    halo_recv,
    lev_send,
    lev_recv,
    out_sem,
):
    loads = []
    for i, (hbm, ref) in enumerate(
        (
            (src_hbm, src_ref),
            (slots_hbm, slots_ref),
            (col_hbm, col_ref),
            (wt_hbm, wt_ref),
            (cnt_hbm, cnt_ref),
            (near_hbm, near_ref),
            (land_hbm, land_ref),
            (diff_hbm, diff_ref),
        )
    ):
        load = pltpu.make_async_copy(hbm, ref, in_sem.at[i])
        load.start()
        loads.append(load)
    dense = {R: (own_dense, 0)}
    for i, offset in enumerate(ORDER):
        dense[offset] = ((near_dense, far_dense)[i // 2], (i % 2) * SET)
    rows = fields * levels
    targets = land_ref.shape[1]
    tiles = targets // TILE
    f32, bf16 = jnp.float32, jnp.bfloat16
    nd = lax.axis_size("dom")
    nl = lax.axis_size("lev")
    me = lax.axis_index("dom")
    lev = lax.axis_index("lev")

    def at(step):
        return lax.rem(me + step + nd, nd)

    barrier = pltpu.get_barrier_semaphore()
    for step in (-2, -1, 1, 2):
        pl.semaphore_signal(barrier, inc=1, device_id=(at(step), lev), device_id_type=MESH)

    @pl.when(lev > 0)
    def _():
        pl.semaphore_signal(barrier, inc=1, device_id=(me, lev - 1), device_id_type=MESH)

    @pl.when(lev < nl - 1)
    def _():
        pl.semaphore_signal(barrier, inc=1, device_id=(me, lev + 1), device_id_type=MESH)

    def pick(offset):
        for c in range(CAP):
            slot = slots_ref[0, offset, c]
            outbox[offset, :, c * B : (c + 1) * B] = blocks[slot]

    loads[0].wait()
    loads[1].wait()
    for block in range(src_ref.shape[1] // B):
        blocks[block] = src_ref[:, block * B : (block + 1) * B]
    for offset in ORDER:
        pick(offset)
    beside_count = jnp.where(lev > 0, 1, 0) + jnp.where(lev < nl - 1, 1, 0)
    pl.semaphore_wait(barrier, 4 + beside_count)

    copies = []
    for i, offset in enumerate(ORDER):
        copy = pltpu.make_async_remote_copy(
            src_ref=outbox.at[offset],
            dst_ref=inbox.at[i // 2, :, pl.ds((i % 2) * SET, SET)],
            send_sem=send_sem.at[i],
            recv_sem=recv_sem.at[i],
            device_id=(at(offset - R), lev),
            device_id_type=MESH,
        )
        copy.start()
        copies.append(copy)
    pick(R)

    for load in loads[2:]:
        load.wait()
    slot_ids = lax.broadcasted_iota(jnp.int32, (K, targets), 0)
    live = jnp.where(slot_ids < cnt_ref[...], wt_ref[...], 0.0)
    share_ref[...] = (live / jnp.sum(live, axis=0, keepdims=True)).astype(bf16).astype(f32)

    row16 = lax.broadcasted_iota(jnp.int32, (16, B), 0).astype(f32)

    def strip_of(s):
        return pl.ds(pl.multiple_of(s * B, B), B)

    def build(offset, s):
        target, low_row = dense[offset]
        lanes = strip_of(s)
        col = col_ref[:, lanes].astype(f32)
        share = share_ref[:, lanes]
        shares = [jnp.broadcast_to(share[k : k + 1], (16, B)).astype(bf16) for k in range(K)]
        for h in range(SET // HALF):
            base = float(offset * SET + h * HALF)
            places = [
                jnp.broadcast_to(col[k : k + 1] - base, (16, B)).astype(bf16) for k in range(K)
            ]
            for i in range(HALF // 16):
                ids = (row16 + float(16 * i)).astype(bf16)
                acc = jnp.zeros((16, B), bf16)
                for k in range(K):
                    acc = jnp.where(places[k] == ids, shares[k], acc)
                start = low_row + h * HALF + 16 * i
                target[start : start + 16, lanes] = acc

    def build_near(s):
        lanes = strip_of(s)
        start = (s // (TILE // B)) * TILE
        near = (near_ref[:, lanes] - start).astype(f32)
        one = jnp.ones((16, B), bf16)
        for h in range(2):
            places = [
                jnp.broadcast_to(near[n : n + 1] - float(h * HALF), (16, B)).astype(bf16)
                for n in range(NN)
            ]
            for i in range(HALF // 16):
                ids = (row16 + float(16 * i)).astype(bf16)
                acc = jnp.zeros((16, B), bf16)
                for n in range(NN):
                    acc = jnp.where(places[n] == ids, acc + one, acc)
                at_row = h * HALF + 16 * i
                wref[at_row : at_row + 16, lanes] = acc

    def tile_of(j, shift=0, width=TILE):
        return pl.ds(pl.multiple_of(j * TILE + shift, B), width)

    def product(part, j):
        if part == 0:
            left, right = outbox[R], own_dense
        else:
            left, right = inbox[part - 1], (near_dense, far_dense)[part - 1]
        return jnp.dot(left, right[:, tile_of(j)], preferred_element_type=f32)

    def loop(body, low, high, group=1):
        def step(i, carry):
            for p in range(group):
                body(low + i * group + p)
            return carry

        lax.fori_loop(0, (high - low) // group, step, 0)

    both = TILE // B

    def build_tile(offset, j):
        for p in range(both):
            build(offset, j * both + p)

    def near_tile(j):
        for p in range(both):
            build_near(j * both + p)

    for part in range(rows // TILE):
        row_id = lax.broadcasted_iota(jnp.int32, (TILE, rows), 0) + part * TILE
        col_id = lax.broadcasted_iota(jnp.int32, (TILE, rows), 1)
        beside = (jnp.abs(row_id - col_id) == 1) & (row_id // levels == col_id // levels)
        tri_ref[part * TILE : (part + 1) * TILE, :] = jnp.where(beside, 1.0, 0.0).astype(bf16)
    lane_id = lax.broadcasted_iota(jnp.int32, (levels, levels), 1)
    level_id = lax.broadcasted_iota(jnp.int32, (levels, levels), 0)
    for f in range(fields):
        spread = jnp.broadcast_to(diff_ref[f : f + 1, :], (levels, levels))
        column = jnp.sum(jnp.where(lane_id == level_id, spread, 0.0), axis=1, keepdims=True)
        dref[f * levels : (f + 1) * levels, :] = jnp.broadcast_to(column, (levels, TILE))
    first_row = lax.broadcasted_iota(jnp.int32, (16, targets), 0) == 0
    ocean_row = jnp.broadcast_to(land_ref[...].astype(f32), (16, targets))
    xm[rows:, H : H + targets] = jnp.where(first_row, ocean_row, 0.0).astype(bf16)

    def own_first(j):
        rref[:, tile_of(j)] = product(0, j)
        build_tile(ORDER[0], j)

    def second(j):
        rref[:, tile_of(j)] += product(1, j)
        build_tile(ORDER[3], j)

    loop(lambda j: build_tile(R, j), 0, tiles)
    loop(own_first, 0, tiles, 2)
    loop(near_tile, 0, tiles)
    loop(lambda j: build_tile(ORDER[1], j), 0, tiles)
    loop(lambda j: build_tile(ORDER[2], j), 0, tiles)
    copies[0].wait_recv()
    copies[1].wait_recv()
    loop(second, 0, tiles, 2)
    copies[2].wait_recv()
    copies[3].wait_recv()

    def last(j):
        value = rref[:, tile_of(j)] + product(2, j)
        rref[:, tile_of(j)] = value
        ocean = land_ref[:, tile_of(j)].astype(f32)
        xm[:rows, tile_of(j, H)] = (value * ocean).astype(bf16)
        for side, level in ((0, levels - 1), (1, 0)):
            picked = [
                rref[f * levels + level : f * levels + level + 1, tile_of(j, p * B, B)]
                for p in range(both)
                for f in range(fields)
            ]
            lev_out[side, :, strip_of(j)] = jnp.concatenate(picked, axis=0).astype(bf16)

    last(0)
    last(tiles - 1)
    halos = []
    for i, (start, landing, step) in enumerate(
        ((targets, 0, 1), (H, H + targets, -1))
    ):
        copy = pltpu.make_async_remote_copy(
            src_ref=xm.at[:, pl.ds(start, H)],
            dst_ref=xm.at[:, pl.ds(landing, H)],
            send_sem=halo_send.at[i],
            recv_sem=halo_recv.at[i],
            device_id=(at(step), lev),
            device_id_type=MESH,
        )
        copy.start()
        halos.append(copy)
    loop(last, 1, tiles - 1, 7)

    def level_copy(side):
        return pltpu.make_async_remote_copy(
            src_ref=lev_out.at[side],
            dst_ref=lev_in.at[side],
            send_sem=lev_send.at[side],
            recv_sem=lev_recv.at[side],
            device_id=(me, lev + 1 if side == 0 else lev - 1),
            device_id_type=MESH,
        )

    @pl.when(lev < nl - 1)
    def _():
        level_copy(0).start()

    @pl.when(lev > 0)
    def _():
        level_copy(1).start()

    @pl.when(lev == 0)
    def _():
        lev_in[0] = jnp.zeros(lev_in.shape[1:], bf16)

    @pl.when(lev == nl - 1)
    def _():
        lev_in[1] = jnp.zeros(lev_in.shape[1:], bf16)

    def final(j):
        gathered = jnp.dot(
            xm[:, tile_of(j, 0, 2 * TILE)], wref[:, tile_of(j)], preferred_element_type=f32
        )
        value = rref[:, tile_of(j)]
        beside = jnp.dot(tri_ref[...], value.astype(bf16), preferred_element_type=f32)
        d = dref[...]
        total = gathered[rows : rows + 1]
        ocean = land_ref[:, tile_of(j)].astype(f32)
        rref[:, tile_of(j)] = ocean * (
            value * ((1.0 - 2.0 * vertical_rate) - d * total)
            + d * gathered[:rows]
            + vertical_rate * beside
        )

    def out_copy(j):
        return pltpu.make_async_copy(
            qref.at[:, tile_of(j)], out_ref.at[:, tile_of(j)], out_sem.at[j]
        )

    def edges(j):
        for side, level in ((0, 0), (1, levels - 1)):
            part = lev_in[side, :, strip_of(j)].astype(f32)
            for p in range(both):
                for f in range(fields):
                    row = f * levels + level
                    at_part = p * fields + f
                    edge = part[at_part : at_part + 1]
                    lanes = tile_of(j, p * B, B)
                    ocean = vertical_rate * land_ref[:, lanes].astype(f32)
                    rref[row : row + 1, lanes] += ocean * edge
        qref[:, tile_of(j)] = rref[:, tile_of(j)].astype(bf16)
        out_copy(j).start()

    middle = tiles // 2 - 1
    loop(final, 1, middle, 3)

    @pl.when(lev > 0)
    def _():
        level_copy(0).wait_recv()
        level_copy(1).wait_send()

    @pl.when(lev < nl - 1)
    def _():
        level_copy(1).wait_recv()
        level_copy(0).wait_send()

    def finish(j):
        final(j)
        edges(j)

    loop(edges, 1, middle)
    loop(finish, middle, tiles - 1, 4)
    for copy in halos:
        copy.wait_recv()
    for copy in halos:
        copy.wait_send()
    finish(0)
    finish(tiles - 1)
    for copy in copies:
        copy.wait_send()
    loop(lambda j: out_copy(j).wait(), 0, tiles)


def on_device(
    source,
    send_slots,
    intersection_col,
    intersection_wt,
    intersection_count,
    neighbours,
    land_mask,
    diffusivity,
):
    fields, levels, columns = source.shape
    rows = fields * levels
    targets = land_mask.shape[0]
    f32, bf16 = jnp.float32, jnp.bfloat16
    land = land_mask.reshape(1, targets)
    result = pl.pallas_call(
        functools.partial(kernel, fields, levels),
        out_shape=jax.ShapeDtypeStruct((rows, targets), bf16),
        in_specs=[pl.BlockSpec(memory_space=pltpu.HBM)] * 8,
        out_specs=pl.BlockSpec(memory_space=pl.ANY),
        scratch_shapes=[
            pltpu.SMEM(send_slots.shape, jnp.int32),
            pltpu.VMEM((rows, columns), bf16),
            pltpu.VMEM((K, targets), jnp.int32),
            pltpu.VMEM((K, targets), f32),
            pltpu.VMEM((1, targets), jnp.int32),
            pltpu.VMEM((NN, targets), jnp.int32),
            pltpu.VMEM((1, targets), jnp.int32),
            pltpu.VMEM((fields, levels), f32),
            pltpu.SemaphoreType.DMA((8,)),
            pltpu.VMEM((columns // B, rows, B), bf16),
            pltpu.VMEM((OFFS, rows, SET), bf16),
            pltpu.VMEM((2, rows, 2 * SET), bf16),
            pltpu.VMEM((SET, targets), bf16),
            pltpu.VMEM((2 * SET, targets), bf16),
            pltpu.VMEM((2 * SET, targets), bf16),
            pltpu.VMEM((2 * TILE, targets), bf16),
            pltpu.VMEM((K, targets), f32),
            pltpu.VMEM((rows, targets), f32),
            pltpu.VMEM((rows, targets), bf16),
            pltpu.VMEM((rows + 16, targets + 2 * H), bf16),
            pltpu.VMEM((rows, rows), bf16),
            pltpu.VMEM((rows, TILE), f32),
            pltpu.VMEM((2, 2 * fields, targets // 2), bf16),
            pltpu.VMEM((2, 2 * fields, targets // 2), bf16),
            pltpu.SemaphoreType.DMA((OFFS - 1,)),
            pltpu.SemaphoreType.DMA((OFFS - 1,)),
            pltpu.SemaphoreType.DMA((2,)),
            pltpu.SemaphoreType.DMA((2,)),
            pltpu.SemaphoreType.DMA((2,)),
            pltpu.SemaphoreType.DMA((2,)),
            pltpu.SemaphoreType.DMA((targets // TILE,)),
        ],
        compiler_params=pltpu.CompilerParams(
            collective_id=0, has_side_effects=True, vmem_limit_bytes=64 * 1024 * 1024
        ),
    )(
        send_slots,
        source.reshape(rows, columns),
        intersection_col,
        intersection_wt,
        intersection_count.reshape(1, targets),
        neighbours,
        land,
        diffusivity,
    )
    return result.astype(f32).reshape(fields, levels, targets)


def solution(mesh):
    return jax.shard_map(
        on_device,
        mesh=mesh,
        in_specs=(
            P(None, "lev", "dom"),
            P("dom", None, None),
            P(None, "dom"),
            P(None, "dom"),
            P("dom"),
            P(None, "dom"),
            P("dom"),
            P(None, "lev"),
        ),
        out_specs=P(None, "lev", "dom"),
        check_vma=False,
    )
```
